32 devices in a mesh: row: 8 (over z, y), col: 4 (over x, core).
Axes of the slice: x: 2, y: 2, z: 4, core: 2. Of those that a mesh axis runs over, the one named last changes fastest.
Arguments:
- items: bfloat16 [16384, 256], P(('row', 'col')), may hold values from -1.5 to 1.5
- contexts: bfloat16 [8192, 256], P(('col', 'row')), may hold values from -1.5 to 1.5
- tiles: int32 [8, 4, 4, 4], P('row', 'col'), may hold values from 0 to 15, as said below
Outputs:
- item_grads: float32 [16384, 256], P(('row', 'col'))
- context_grads: float32 [8192, 256], P(('col', 'row'))
The draws below stay inside these ranges and needn't reach their ends.
Inputs may be any that keep to these rules, and one draw needn't show every extreme that they name: tiles[r, c] lists 4 distinct tiles whose item block lies in [r * 2, (r + 1) * 2) and context block in [c * 2, (c + 1) * 2); live slots (both counts 1 to 4) come first, empty slots carry counts 0; each index pair holds 1 to 4 live slots, and the pair 0, 0 holds 4.
All inputs are finite; a program needn't handle non-finite values.
Results may differ from the reference program's by a relative error of at most 0.00042.
Values may be sent and summed in bfloat16 or wider, within the bound.
A program may use at most 64 MiB of HBM per device.

```python
import jax
import jax.numpy as jnp
from jax import lax

D = 256
TILE = 1024
RB = 2
CB = 2
SLOTS = 4
NI = 16384
NC = 8192
N_ROW = 8
N_COL = 4


def draw_tiles(key, part):
    devices_all = N_ROW * N_COL
    key_perm, key_live, key_pos, key_neg = jax.random.split(key, 4)
    perm_keys = jax.random.split(key_perm, devices_all)
    chosen = jax.vmap(lambda k: jax.random.permutation(k, RB * CB))(perm_keys)[:, :SLOTS]
    device_ids = jnp.arange(devices_all, dtype=jnp.int32)
    slot_order = jnp.arange(SLOTS, dtype=jnp.int32)[None, :]
    chosen = jnp.where(device_ids[:, None] == 0, slot_order, chosen)
    chosen = jnp.where(device_ids[:, None] == devices_all - 1, RB * CB - 1 - slot_order, chosen)
    live = jax.random.randint(key_live, (devices_all,), 1, SLOTS + 1)
    live = jnp.where(device_ids == 0, SLOTS, live)
    active = slot_order < live[:, None]
    positive = jnp.where(active, jax.random.randint(key_pos, (devices_all, SLOTS), 1, 5), 0)
    negative = jnp.where(active, jax.random.randint(key_neg, (devices_all, SLOTS), 1, 5), 0)
    row_index = device_ids // N_COL
    col_index = device_ids % N_COL
    row_block = row_index[:, None] * RB + chosen // CB
    col_block = col_index[:, None] * CB + chosen % CB
    table = jnp.stack([row_block, col_block, positive, negative], axis=-1).astype(jnp.int32)
    return table.reshape(N_ROW, N_COL, SLOTS, 4)


def shard_levels(stream_key, extent, cuts, low, largest):
    def one(axis_at, blocks):
        draws = jax.random.uniform(jax.random.fold_in(jax.random.fold_in(stream_key, 6), axis_at), (blocks,), jnp.float32, low / len(cuts), largest / len(cuts))
        return jnp.repeat(jnp.exp(draws), extent[axis_at] // blocks).reshape((-1,) + (1,) * (len(extent) - axis_at - 1))

    loudness = one(*cuts[0])
    for cut in cuts[1:]:
        loudness = loudness * one(*cut)
    return loudness


def bell_draw(stream_key, shape, width, most, pieces=(), kind=jnp.bfloat16):
    factor_of = shard_levels(stream_key, shape, pieces, -0.22, 0.18) if pieces else 1.0
    array = jax.random.normal(stream_key, shape, jnp.float32) * width * factor_of
    return jnp.minimum(jnp.maximum(array, -most), most).astype(kind)


def setup_inputs(seed: int = 0) -> dict:
    key_of = jax.random.split(jax.random.key(seed), 4)
    return {
        "items": bell_draw(key_of[0], (NI, D), 0.25, 1.5, ((0, 32),)),
        "contexts": bell_draw(key_of[1], (NC, D), 0.25, 1.5, ((0, 32),)),
        "tiles": draw_tiles(jax.random.fold_in(key_of[3], 71), 0),
    }


def reference(items, contexts, tiles):
    flat = tiles.reshape(-1, 4)
    factor = 1.0 / (TILE ** 0.5)

    def advance(carry, entry):
        grad_items, grad_contexts = carry
        row_start = (entry[0] * TILE).astype(jnp.int32)
        col_start = (entry[1] * TILE).astype(jnp.int32)
        item_block = lax.dynamic_slice_in_dim(items, row_start, TILE, 0)
        context_block = lax.dynamic_slice_in_dim(contexts, col_start, TILE, 0)
        scores = jnp.dot(item_block, context_block.T, preferred_element_type=jnp.float32)
        positive = entry[2].astype(jnp.float32)
        negative = entry[3].astype(jnp.float32)
        resid = (((positive + negative) * jax.nn.sigmoid(scores) - positive) * factor).astype(jnp.bfloat16)
        item_term = jnp.dot(resid, context_block, preferred_element_type=jnp.float32)
        context_term = jnp.dot(resid.T, item_block, preferred_element_type=jnp.float32)
        old_items = lax.dynamic_slice_in_dim(grad_items, row_start, TILE, 0)
        grad_items = lax.dynamic_update_slice_in_dim(grad_items, old_items + item_term, row_start, 0)
        old_contexts = lax.dynamic_slice_in_dim(grad_contexts, col_start, TILE, 0)
        grad_contexts = lax.dynamic_update_slice_in_dim(grad_contexts, old_contexts + context_term, col_start, 0)
        return (grad_items, grad_contexts), None

    start = (jnp.zeros(items.shape, jnp.float32), jnp.zeros(contexts.shape, jnp.float32))
    (grad_items, grad_contexts), _ = lax.scan(advance, start, flat)
    return grad_items, grad_contexts
```

```python
import functools

import jax
import jax.numpy as jnp
from jax import lax
from jax.experimental import pallas as pl
from jax.experimental.pallas import tpu as pltpu
from jax.sharding import PartitionSpec as P

TILE = 1024
RB = 2
CB = 2
SLOTS = 4


def kernel(
    nr, nc, items_ref, ctx_ref, tiles_ref, gi_out, gc_out,
    items_all, ctx_all, gi, gco, gcs, ry, rz, rk, rx, coef,
    s_ic, r_ic, s_ix, r_ix, s_ir, r_ir, s_cy, r_cy, s_cz, r_cz, s_cr, r_cr,
    s_gy, r_gy, s_gz, r_gz, s_ik, r_ik, s_xx, r_xx,
):
    nz, nx = nr // 2, nc // 2
    bi, bc = items_ref.shape[0], ctx_ref.shape[0]
    r = lax.axis_index("row")
    c = lax.axis_index("col")
    z, y = r // 2, r % 2
    x, k = c // 2, c % 2

    def dev(zz, yy, xx, kk):
        return (zz * 2 + yy, xx * 2 + kk)

    def zof(d):
        return lax.rem(z + d, nz)

    def xof(d):
        return lax.rem(x + d, nx)

    ypeer = dev(z, 1 - y, x, k)
    kpeer = dev(z, y, x, 1 - k)

    barrier = pltpu.get_barrier_semaphore()
    peers = [kpeer, ypeer]
    peers += [dev(z, y, xof(e), k) for e in range(1, nx)]
    peers += [dev(zof(e), y, x, k) for e in range(1, nz)]
    for p in peers:
        pl.semaphore_signal(barrier, inc=1, device_id=p, device_id_type=pl.DeviceIdType.MESH)
    pl.semaphore_wait(barrier, len(peers))

    def rcopy(src, dst, ss, rs, to):
        return pltpu.make_async_remote_copy(
            src_ref=src, dst_ref=dst, send_sem=ss, recv_sem=rs,
            device_id=to, device_id_type=pl.DeviceIdType.MESH,
        )

    def islot(i):
        return items_all.at[pl.ds(pl.multiple_of(i * bi, bi), bi)]

    def cslot(j):
        return ctx_all.at[pl.ds(pl.multiple_of(j * bc, bc), bc)]

    c_ic = rcopy(items_ref, islot(c), s_ic, r_ic, kpeer)
    c_cy = rcopy(ctx_ref, cslot(r), s_cy, r_cy, ypeer)

    def c_ix(e):
        return rcopy(items_ref, islot(c), s_ix.at[e], r_ix.at[nx - e], dev(z, y, xof(e), k))

    def c_cz(e):
        return rcopy(ctx_ref, cslot(r), s_cz.at[e], r_cz.at[nz - e], dev(zof(e), y, x, k))

    def c_ir(d):
        blk = islot(xof(d) * 2 + k)
        return rcopy(blk, blk, s_ir.at[d], r_ir.at[d], kpeer)

    def c_cr(d):
        blk = cslot(zof(d) * 2 + y)
        return rcopy(blk, blk, s_cr.at[d], r_cr.at[d], ypeer)

    c_ic.start()
    for e in range(1, nx):
        c_ix(e).start()
    for e in range(1, nz):
        c_cz(e).start()
    c_cy.start()

    items_all[pl.ds(pl.multiple_of(c * bi, bi), bi), :] = items_ref[...]
    ctx_all[pl.ds(pl.multiple_of(r * bc, bc), bc), :] = ctx_ref[...]

    for a in range(RB):
        for b in range(CB):
            pos = jnp.int32(0)
            neg = jnp.int32(0)
            for s in range(SLOTS):
                hit = (tiles_ref[0, 0, s, 0] == r * RB + a) & (tiles_ref[0, 0, s, 1] == c * CB + b)
                pos = pos + jnp.where(hit, tiles_ref[0, 0, s, 2], 0)
                neg = neg + jnp.where(hit, tiles_ref[0, 0, s, 3], 0)
            half = 0.5 / TILE**0.5
            coef[2 * (a * CB + b)] = (pos + neg).astype(jnp.float32) * half
            coef[2 * (a * CB + b) + 1] = (neg - pos).astype(jnp.float32) * half

    def unit(i, j, dst, first_c, first_i):
        cb = ctx_all[pl.ds(pl.multiple_of(j * bc, bc), bc), :]
        rows = pl.ds(pl.multiple_of(i * bi, bi), bi)
        ib = items_all[rows, :]
        at = 2 * ((i // (nc // RB)) * CB + j // (nr // CB))
        amp = coef[at]
        off = coef[at + 1]
        sc = lax.dot_general(ib, cb, (((1,), (1,)), ((), ())), preferred_element_type=jnp.float32)
        res = (jnp.tanh(sc * 0.5) * amp + off).astype(jnp.bfloat16)
        it = jnp.dot(res, cb, preferred_element_type=jnp.float32)
        ct = lax.dot_general(res, ib, (((0,), (0,)), ((), ())), preferred_element_type=jnp.float32)
        if first_i:
            gi[rows, :] = it
        else:
            gi[rows, :] += it
        if first_c:
            dst[...] = ct
        else:
            dst[...] += ct

    def block(j, dst, first_i=False):
        unit(c, j, dst, True, first_i)
        unit(x * 2 + 1 - k, j, dst, False, first_i)

        def step(e, carry):
            unit(xof(e) * 2 + k, j, dst, False, first_i)
            unit(xof(e) * 2 + 1 - k, j, dst, False, first_i)
            return carry

        lax.fori_loop(1, nx, step, 0, unroll=nx <= 2)

    def c_gy(d):
        return rcopy(gcs.at[d], ry.at[d], s_gy.at[d], r_gy.at[d], ypeer)

    def c_gz(d):
        return rcopy(gco.at[d], rz.at[nz - d], s_gz.at[d], r_gz.at[nz - d], dev(zof(d), y, x, k))

    def flush(d):
        c_gy(d).wait_recv()
        gco[d] += ry[d]
        c_gz(d).start()

    first = gco.at[0]
    unit(c, r, first, True, True)
    c_ic.wait_recv()
    unit(x * 2 + 1 - k, r, first, False, True)
    for e in range(1, nx):
        c_ix(nx - e).wait_recv()
        c_ir(e).start()
        unit(xof(e) * 2 + k, r, first, False, True)
    c_cz(nz - 1).wait_recv()
    c_cr(1).start()
    for e in range(1, nx):
        c_ir(e).wait_recv()
        unit(xof(e) * 2 + 1 - k, r, first, False, True)
    c_cy.wait_recv()
    block(z * 2 + 1 - y, gcs.at[0])
    c_gy(0).start()

    def zstep(d, carry):
        block(zof(d) * 2 + y, gco.at[d])

        @pl.when(d + 1 < nz)
        def _():
            c_cz(nz - 1 - d).wait_recv()
            c_cr(d + 1).start()

        c_cr(d).wait_recv()
        block(zof(d) * 2 + 1 - y, gcs.at[d])
        c_gy(d).start()

        @pl.when(d > 1)
        def _():
            flush(d - 1)

        return carry

    lax.fori_loop(1, nz, zstep, 0)

    def c_ik(e):
        rows = pl.ds(pl.multiple_of((xof(e) * 2 + 1 - k) * bi, bi), bi)
        return rcopy(gi.at[rows], rk.at[e], s_ik.at[e], r_ik.at[e], kpeer)

    def c_xx(e):
        rows = pl.ds(pl.multiple_of((xof(e) * 2 + k) * bi, bi), bi)
        return rcopy(gi.at[rows], rx.at[nx - e], s_xx.at[e], r_xx.at[nx - e], dev(z, y, xof(e), k))

    order = list(range(1, nx)) + [0]
    for e in order:
        c_ik(e).start()
    for e in range(1, nx):
        c_ik(e).wait_recv()
        rows = pl.ds(pl.multiple_of((xof(e) * 2 + k) * bi, bi), bi)
        gi[rows, :] += rk[e]
        c_xx(e).start()
    flush(nz - 1)

    c_ik(0).wait_recv()
    acc_i = gi[pl.ds(pl.multiple_of(c * bi, bi), bi), :] + rk[0]
    gi_out[...] = acc_i
    c_gy(0).wait_recv()
    gc_out[...] = gco[0] + ry[0]
    for e in range(1, nz):
        c_gz(nz - e).wait_recv()
        gc_out[...] += rz[e]
    for e in range(1, nx):
        c_xx(nx - e).wait_recv()
        gi_out[...] += rx[e]

    c_ic.wait_send()
    c_cy.wait_send()
    c_gy(0).wait_send()
    c_ik(0).wait_send()
    for e in range(1, nx):
        c_ix(e).wait_send()
        c_ir(e).wait_send()
        c_ik(e).wait_send()
        c_xx(e).wait_send()
    for e in range(1, nz):
        c_cz(e).wait_send()
        c_cr(e).wait_send()
        c_gy(e).wait_send()
        c_gz(e).wait_send()


def shards(nr, nc, items, contexts, tiles):
    bi, dim = items.shape
    bc = contexts.shape[0]
    nz, nx = nr // 2, nc // 2
    f32 = jnp.float32
    dma = pltpu.SemaphoreType.DMA
    pairs = [(), (nx,), (nx,), (), (nz,), (nz,), (nz,), (nz,), (nx,), (nx,)]
    sems = []
    for shape in pairs:
        sems += [dma(shape) if shape else dma] * 2
    vm = pl.BlockSpec(memory_space=pltpu.VMEM)
    return pl.pallas_call(
        functools.partial(kernel, nr, nc),
        out_shape=(
            jax.ShapeDtypeStruct((bi, dim), f32),
            jax.ShapeDtypeStruct((bc, dim), f32),
        ),
        in_specs=[vm, vm, pl.BlockSpec(memory_space=pltpu.SMEM)],
        out_specs=(vm, vm),
        scratch_shapes=[
            pltpu.VMEM((bi * nc, dim), items.dtype),
            pltpu.VMEM((bc * nr, dim), contexts.dtype),
            pltpu.VMEM((bi * nc, dim), f32),
            pltpu.VMEM((nz, bc, dim), f32),
            pltpu.VMEM((nz, bc, dim), f32),
            pltpu.VMEM((nz, bc, dim), f32),
            pltpu.VMEM((nz, bc, dim), f32),
            pltpu.VMEM((nx, bi, dim), f32),
            pltpu.VMEM((nx, bi, dim), f32),
            pltpu.SMEM((2 * RB * CB,), f32),
        ] + sems,
        compiler_params=pltpu.CompilerParams(
            collective_id=0, has_side_effects=True, vmem_limit_bytes=40 * 2**20
        ),
    )(items, contexts, tiles)


def solution(mesh):
    nr, nc = mesh.shape["row"], mesh.shape["col"]
    placed = (P(("row", "col"), None), P(("col", "row"), None), P("row", "col", None, None))
    return jax.shard_map(
        functools.partial(shards, nr, nc),
        mesh=mesh,
        in_specs=placed,
        out_specs=(P(("row", "col"), None), P(("col", "row"), None)),
        check_vma=False,
    )
```

```python
import functools

import jax
import jax.numpy as jnp
from jax import lax
from jax.experimental import pallas as pl
from jax.experimental.pallas import tpu as pltpu
from jax.sharding import PartitionSpec as P

TILE = 1024
RB = 2
CB = 2
SLOTS = 4
LEVELS = 32766.0


class Both:
    def __init__(self, *copies):
        self.copies = copies

    def start(self):
        for one in self.copies:
            one.start()

    def wait_recv(self):
        for one in self.copies:
            one.wait_recv()

    def wait_send(self):
        for one in self.copies:
            one.wait_send()


def encode(value, codes, peaks):
    rows, dim = value.shape
    cube = value.reshape(rows // 8, 8, dim)
    peak = jnp.maximum(jnp.max(jnp.abs(cube), axis=0), 1e-30)
    peaks[...] = peak * (1.0 / LEVELS)
    scaled = jnp.round(cube * (LEVELS / peak)[None]).reshape(rows, dim)
    codes[...] = scaled.astype(jnp.int32).astype(jnp.int16)


def decode(codes, peaks):
    rows, dim = codes.shape
    cube = codes.astype(jnp.int32).astype(jnp.float32).reshape(rows // 8, 8, dim)
    return (cube * peaks[None]).reshape(rows, dim)


def kernel(
    nr, nc, items_ref, ctx_ref, tiles_ref, gi_out, gc_out,
    items_all, ctx_all, gi, gco, gct, coef,
    qy, ry, qz, rz, qk, rk, qx, rx, my, ny, mz, nz_, mk, nk, mx, nx_,
    s_ic, r_ic, s_ix, r_ix, s_ir, r_ir, s_cy, r_cy, s_cz, r_cz, s_cr, r_cr,
    s_gy, r_gy, s_gz, r_gz, s_ik, r_ik, s_xx, r_xx,
    s_my, r_my, s_mz, r_mz, s_mk, r_mk, s_mx, r_mx,
):
    nz, nx = nr // 2, nc // 2
    bi, bc = items_ref.shape[0], ctx_ref.shape[0]
    r = lax.axis_index("row")
    c = lax.axis_index("col")
    z, y = r // 2, r % 2
    x, k = c // 2, c % 2

    def dev(zz, yy, xx, kk):
        return (zz * 2 + yy, xx * 2 + kk)

    def zof(d):
        return lax.rem(z + d, nz)

    def xof(d):
        return lax.rem(x + d, nx)

    ypeer = dev(z, 1 - y, x, k)
    kpeer = dev(z, y, x, 1 - k)

    barrier = pltpu.get_barrier_semaphore()
    peers = [kpeer, ypeer]
    peers += [dev(z, y, xof(e), k) for e in range(1, nx)]
    peers += [dev(zof(e), y, x, k) for e in range(1, nz)]
    for p in peers:
        pl.semaphore_signal(barrier, inc=1, device_id=p, device_id_type=pl.DeviceIdType.MESH)
    pl.semaphore_wait(barrier, len(peers))

    def rcopy(src, dst, ss, rs, to):
        return pltpu.make_async_remote_copy(
            src_ref=src, dst_ref=dst, send_sem=ss, recv_sem=rs,
            device_id=to, device_id_type=pl.DeviceIdType.MESH,
        )

    def islot(i):
        return items_all.at[pl.ds(pl.multiple_of(i * bi, bi), bi)]

    def cslot(j):
        return ctx_all.at[pl.ds(pl.multiple_of(j * bc, bc), bc)]

    c_ic = rcopy(items_ref, islot(c), s_ic, r_ic, kpeer)
    c_cy = rcopy(ctx_ref, cslot(r), s_cy, r_cy, ypeer)

    def c_ix(e):
        return rcopy(items_ref, islot(c), s_ix.at[e], r_ix.at[nx - e], dev(z, y, xof(e), k))

    def c_cz(e):
        return rcopy(ctx_ref, cslot(r), s_cz.at[e], r_cz.at[nz - e], dev(zof(e), y, x, k))

    def c_ir(d):
        blk = islot(xof(d) * 2 + k)
        return rcopy(blk, blk, s_ir.at[d], r_ir.at[d], kpeer)

    def c_cr(d):
        blk = cslot(zof(d) * 2 + y)
        return rcopy(blk, blk, s_cr.at[d], r_cr.at[d], ypeer)

    c_ic.start()
    for e in range(1, nx):
        c_ix(e).start()
    for e in range(1, nz):
        c_cz(e).start()
    c_cy.start()

    items_all[pl.ds(pl.multiple_of(c * bi, bi), bi), :] = items_ref[...]
    ctx_all[pl.ds(pl.multiple_of(r * bc, bc), bc), :] = ctx_ref[...]

    for a in range(RB):
        for b in range(CB):
            pos = jnp.int32(0)
            neg = jnp.int32(0)
            for s in range(SLOTS):
                hit = (tiles_ref[0, 0, s, 0] == r * RB + a) & (tiles_ref[0, 0, s, 1] == c * CB + b)
                pos = pos + jnp.where(hit, tiles_ref[0, 0, s, 2], 0)
                neg = neg + jnp.where(hit, tiles_ref[0, 0, s, 3], 0)
            half = 0.5 / TILE**0.5
            coef[2 * (a * CB + b)] = (pos + neg).astype(jnp.float32) * half
            coef[2 * (a * CB + b) + 1] = (neg - pos).astype(jnp.float32) * half

    def unit(i, j, dst, first_c, first_i):
        cb = ctx_all[pl.ds(pl.multiple_of(j * bc, bc), bc), :]
        rows = pl.ds(pl.multiple_of(i * bi, bi), bi)
        ib = items_all[rows, :]
        at = 2 * ((i // (nc // RB)) * CB + j // (nr // CB))
        amp = coef[at]
        off = coef[at + 1]
        sc = lax.dot_general(ib, cb, (((1,), (1,)), ((), ())), preferred_element_type=jnp.float32)
        res = (jnp.tanh(sc * 0.5) * amp + off).astype(jnp.bfloat16)
        it = jnp.dot(res, cb, preferred_element_type=jnp.float32)
        ct = lax.dot_general(res, ib, (((0,), (0,)), ((), ())), preferred_element_type=jnp.float32)
        if first_i:
            gi[rows, :] = it
        else:
            gi[rows, :] += it
        if first_c:
            dst[...] = ct
        else:
            dst[...] += ct

    def block(j, dst, first_i=False):
        unit(c, j, dst, True, first_i)
        unit(x * 2 + 1 - k, j, dst, False, first_i)

        def step(e, carry):
            unit(xof(e) * 2 + k, j, dst, False, first_i)
            unit(xof(e) * 2 + 1 - k, j, dst, False, first_i)
            return carry

        lax.fori_loop(1, nx, step, 0, unroll=nx <= 2)

    def c_gy(d):
        return Both(
            rcopy(qy.at[d], ry.at[d], s_gy.at[d], r_gy.at[d], ypeer),
            rcopy(my.at[d], ny.at[d], s_my.at[d], r_my.at[d], ypeer),
        )

    def c_gz(d):
        to, e = dev(zof(d), y, x, k), nz - d
        return Both(
            rcopy(qz.at[d], rz.at[e], s_gz.at[d], r_gz.at[e], to),
            rcopy(mz.at[d], nz_.at[e], s_mz.at[d], r_mz.at[e], to),
        )

    def flush(d):
        c_gy(d).wait_recv()
        encode(gco[d] + decode(ry[d], ny[d]), qz.at[d], mz.at[d])
        c_gz(d).start()

    first = gco.at[0]
    unit(c, r, first, True, True)
    c_ic.wait_recv()
    unit(x * 2 + 1 - k, r, first, False, True)
    for e in range(1, nx):
        c_ix(nx - e).wait_recv()
        c_ir(e).start()
        unit(xof(e) * 2 + k, r, first, False, True)
    c_cz(nz - 1).wait_recv()
    c_cr(1).start()
    for e in range(1, nx):
        c_ir(e).wait_recv()
        unit(xof(e) * 2 + 1 - k, r, first, False, True)
    c_cy.wait_recv()
    block(z * 2 + 1 - y, gct)
    encode(gct[...], qy.at[0], my.at[0])
    c_gy(0).start()

    def zstep(d, carry):
        block(zof(d) * 2 + y, gco.at[d])

        @pl.when(d + 1 < nz)
        def _():
            c_cz(nz - 1 - d).wait_recv()
            c_cr(d + 1).start()

        c_cr(d).wait_recv()
        block(zof(d) * 2 + 1 - y, gct)
        encode(gct[...], qy.at[d], my.at[d])
        c_gy(d).start()

        @pl.when(d > 1)
        def _():
            flush(d - 1)

        return carry

    lax.fori_loop(1, nz, zstep, 0)

    def rows_of(i):
        return pl.ds(pl.multiple_of(i * bi, bi), bi)

    def c_ik(e):
        return Both(
            rcopy(qk.at[e], rk.at[e], s_ik.at[e], r_ik.at[e], kpeer),
            rcopy(mk.at[e], nk.at[e], s_mk.at[e], r_mk.at[e], kpeer),
        )

    def c_xx(e):
        to, f = dev(z, y, xof(e), k), nx - e
        return Both(
            rcopy(qx.at[e], rx.at[f], s_xx.at[e], r_xx.at[f], to),
            rcopy(mx.at[e], nx_.at[f], s_mx.at[e], r_mx.at[f], to),
        )

    for e in list(range(1, nx)) + [0]:
        encode(gi[rows_of(xof(e) * 2 + 1 - k), :], qk.at[e], mk.at[e])
        c_ik(e).start()
    for e in range(1, nx):
        c_ik(e).wait_recv()
        encode(gi[rows_of(xof(e) * 2 + k), :] + decode(rk[e], nk[e]), qx.at[e], mx.at[e])
        c_xx(e).start()
    flush(nz - 1)

    c_ik(0).wait_recv()
    gi_out[...] = gi[rows_of(c), :] + decode(rk[0], nk[0])
    c_gy(0).wait_recv()
    gc_out[...] = gco[0] + decode(ry[0], ny[0])
    for e in range(1, nz):
        c_gz(nz - e).wait_recv()
        gc_out[...] += decode(rz[e], nz_[e])
    for e in range(1, nx):
        c_xx(nx - e).wait_recv()
        gi_out[...] += decode(rx[e], nx_[e])

    c_ic.wait_send()
    c_cy.wait_send()
    c_gy(0).wait_send()
    c_ik(0).wait_send()
    for e in range(1, nx):
        c_ix(e).wait_send()
        c_ir(e).wait_send()
        c_ik(e).wait_send()
        c_xx(e).wait_send()
    for e in range(1, nz):
        c_cz(e).wait_send()
        c_cr(e).wait_send()
        c_gy(e).wait_send()
        c_gz(e).wait_send()


def shards(nr, nc, items, contexts, tiles):
    bi, dim = items.shape
    bc = contexts.shape[0]
    nz, nx = nr // 2, nc // 2
    f32 = jnp.float32
    dma = pltpu.SemaphoreType.DMA
    pairs = [(), (nx,), (nx,), (), (nz,), (nz,), (nz,), (nz,), (nx,), (nx,)]
    pairs += [(nz,), (nz,), (nx,), (nx,)]
    sems = []
    for shape in pairs:
        sems += [dma(shape) if shape else dma] * 2
    vm = pl.BlockSpec(memory_space=pltpu.VMEM)
    return pl.pallas_call(
        functools.partial(kernel, nr, nc),
        out_shape=(
            jax.ShapeDtypeStruct((bi, dim), f32),
            jax.ShapeDtypeStruct((bc, dim), f32),
        ),
        in_specs=[vm, vm, pl.BlockSpec(memory_space=pltpu.SMEM)],
        out_specs=(vm, vm),
        scratch_shapes=[
            pltpu.VMEM((bi * nc, dim), items.dtype),
            pltpu.VMEM((bc * nr, dim), contexts.dtype),
            pltpu.VMEM((bi * nc, dim), f32),
            pltpu.VMEM((nz, bc, dim), f32),
            pltpu.VMEM((bc, dim), f32),
            pltpu.SMEM((2 * RB * CB,), f32),
        ]
        + [pltpu.VMEM((nz, bc, dim), jnp.int16)] * 4
        + [pltpu.VMEM((nx, bi, dim), jnp.int16)] * 4
        + [pltpu.VMEM((nz, 8, dim), f32)] * 4
        + [pltpu.VMEM((nx, 8, dim), f32)] * 4
        + sems,
        compiler_params=pltpu.CompilerParams(
            collective_id=0, has_side_effects=True, vmem_limit_bytes=40 * 2**20
        ),
    )(items, contexts, tiles)


def solution(mesh):
    nr, nc = mesh.shape["row"], mesh.shape["col"]
    placed = (P(("row", "col"), None), P(("col", "row"), None), P("row", "col", None, None))
    return jax.shard_map(
        functools.partial(shards, nr, nc),
        mesh=mesh,
        in_specs=placed,
        out_specs=(P(("row", "col"), None), P(("col", "row"), None)),
        check_vma=False,
    )
```

```python
import functools

import jax
import jax.numpy as jnp
from jax import lax
from jax.experimental import pallas as pl
from jax.experimental.pallas import tpu as pltpu
from jax.sharding import PartitionSpec as P

TILE = 1024
RB = 2
CB = 2
SLOTS = 4
LEVELS = 32766.0


class Both:
    def __init__(self, *copies):
        self.copies = copies

    def start(self):
        for one in self.copies:
            one.start()

    def wait_recv(self):
        for one in self.copies:
            one.wait_recv()

    def wait_send(self):
        for one in self.copies:
            one.wait_send()


def encode(value, codes, peaks):
    rows, dim = value.shape
    cube = value.reshape(rows // 8, 8, dim)
    peak = jnp.maximum(jnp.max(jnp.abs(cube), axis=0), 1e-30)
    peaks[...] = peak * (1.0 / LEVELS)
    scaled = jnp.round(cube * (LEVELS / peak)[None]).reshape(rows, dim)
    codes[...] = scaled.astype(jnp.int32).astype(jnp.int16)


def decode(codes, peaks):
    rows, dim = codes.shape
    cube = codes.astype(jnp.int32).astype(jnp.float32).reshape(rows // 8, 8, dim)
    return (cube * peaks[None]).reshape(rows, dim)


def kernel(
    nr, nc, items_ref, ctx_ref, tiles_ref, gi_out, gc_out,
    items_all, ctx_all, gi, gco, gct, coef,
    qy, ry, qz, rz, qk, rk, qx, rx, my, ny, mz, nz_, mk, nk, mx, nx_,
    s_ic, r_ic, s_ix, r_ix, s_ir, r_ir, s_cy, r_cy, s_cz, r_cz, s_cr, r_cr,
    s_gy, r_gy, s_gz, r_gz, s_ik, r_ik, s_xx, r_xx,
    s_my, r_my, s_mz, r_mz, s_mk, r_mk, s_mx, r_mx,
):
    nz, nx = nr // 2, nc // 2
    bi, bc = items_ref.shape[0], ctx_ref.shape[0]
    r = lax.axis_index("row")
    c = lax.axis_index("col")
    z, y = r // 2, r % 2
    x, k = c // 2, c % 2

    def dev(zz, yy, xx, kk):
        return (zz * 2 + yy, xx * 2 + kk)

    def zof(d):
        return lax.rem(z + d, nz)

    def xof(d):
        return lax.rem(x + d, nx)

    ypeer = dev(z, 1 - y, x, k)
    kpeer = dev(z, y, x, 1 - k)

    barrier = pltpu.get_barrier_semaphore()
    peers = [kpeer, ypeer]
    peers += [dev(z, y, xof(e), k) for e in range(1, nx)]
    peers += [dev(zof(e), y, x, k) for e in range(1, nz)]
    for p in peers:
        pl.semaphore_signal(barrier, inc=1, device_id=p, device_id_type=pl.DeviceIdType.MESH)
    pl.semaphore_wait(barrier, len(peers))

    def rcopy(src, dst, ss, rs, to):
        return pltpu.make_async_remote_copy(
            src_ref=src, dst_ref=dst, send_sem=ss, recv_sem=rs,
            device_id=to, device_id_type=pl.DeviceIdType.MESH,
        )

    def islot(i):
        return items_all.at[pl.ds(pl.multiple_of(i * bi, bi), bi)]

    def cslot(j):
        return ctx_all.at[pl.ds(pl.multiple_of(j * bc, bc), bc)]

    c_ic = rcopy(items_ref, islot(c), s_ic, r_ic, kpeer)
    c_cy = rcopy(ctx_ref, cslot(r), s_cy, r_cy, ypeer)

    def c_ix(e):
        return rcopy(items_ref, islot(c), s_ix.at[e], r_ix.at[nx - e], dev(z, y, xof(e), k))

    def c_cz(e):
        return rcopy(ctx_ref, cslot(r), s_cz.at[e], r_cz.at[nz - e], dev(zof(e), y, x, k))

    def c_ir(d):
        blk = islot(xof(d) * 2 + k)
        return rcopy(blk, blk, s_ir.at[d], r_ir.at[d], kpeer)

    def c_cr(d):
        blk = cslot(zof(d) * 2 + y)
        return rcopy(blk, blk, s_cr.at[d], r_cr.at[d], ypeer)

    for e in range(1, nx):
        c_ix(e).start()
    c_cz(nz - 1).start()
    c_cy.start()
    c_ic.start()

    items_all[pl.ds(pl.multiple_of(c * bi, bi), bi), :] = items_ref[...]
    ctx_all[pl.ds(pl.multiple_of(r * bc, bc), bc), :] = ctx_ref[...]

    for a in range(RB):
        for b in range(CB):
            pos = jnp.int32(0)
            neg = jnp.int32(0)
            for s in range(SLOTS):
                hit = (tiles_ref[0, 0, s, 0] == r * RB + a) & (tiles_ref[0, 0, s, 1] == c * CB + b)
                pos = pos + jnp.where(hit, tiles_ref[0, 0, s, 2], 0)
                neg = neg + jnp.where(hit, tiles_ref[0, 0, s, 3], 0)
            half = 0.5 / TILE**0.5
            coef[2 * (a * CB + b)] = (pos + neg).astype(jnp.float32) * half
            coef[2 * (a * CB + b) + 1] = (neg - pos).astype(jnp.float32) * half

    def unit(i, j, dst, first_c, first_i):
        cb = ctx_all[pl.ds(pl.multiple_of(j * bc, bc), bc), :]
        rows = pl.ds(pl.multiple_of(i * bi, bi), bi)
        ib = items_all[rows, :]
        at = 2 * ((i // (nc // RB)) * CB + j // (nr // CB))
        amp = coef[at]
        off = coef[at + 1]
        sc = lax.dot_general(ib, cb, (((1,), (1,)), ((), ())), preferred_element_type=jnp.float32)
        res = (jnp.tanh(sc * 0.5) * amp + off).astype(jnp.bfloat16)
        it = jnp.dot(res, cb, preferred_element_type=jnp.float32)
        ct = lax.dot_general(res, ib, (((0,), (0,)), ((), ())), preferred_element_type=jnp.float32)
        if first_i:
            gi[rows, :] = it
        else:
            gi[rows, :] += it
        if first_c:
            dst[...] = ct
        else:
            dst[...] += ct

    def block(j, dst, first_i=False):
        unit(c, j, dst, True, first_i)
        unit(x * 2 + 1 - k, j, dst, False, first_i)

        def step(e, carry):
            unit(xof(e) * 2 + k, j, dst, False, first_i)
            unit(xof(e) * 2 + 1 - k, j, dst, False, first_i)
            return carry

        lax.fori_loop(1, nx, step, 0, unroll=nx <= 2)

    def c_gy(d):
        return Both(
            rcopy(qy.at[d], ry.at[d], s_gy.at[d], r_gy.at[d], ypeer),
            rcopy(my.at[d], ny.at[d], s_my.at[d], r_my.at[d], ypeer),
        )

    def c_gz(d):
        to, e = dev(zof(d), y, x, k), nz - d
        return Both(
            rcopy(qz.at[d], rz.at[e], s_gz.at[d], r_gz.at[e], to),
            rcopy(mz.at[d], nz_.at[e], s_mz.at[d], r_mz.at[e], to),
        )

    def flush(d):
        c_gy(d).wait_recv()
        encode(gco[d] + decode(ry[d], ny[d]), qz.at[d], mz.at[d])
        c_gz(d).start()

    first = gco.at[0]
    unit(c, r, first, True, True)
    c_ic.wait_recv()
    unit(x * 2 + 1 - k, r, first, False, True)
    c_cz(nz - 1).wait_send()
    if nz > 2:
        c_cz(nz - 2).start()
    c_cz(nz - 1).wait_recv()
    c_cr(1).start()
    for e in range(1, nx):
        c_ix(nx - e).wait_recv()
        c_ir(e).start()
        unit(xof(e) * 2 + k, r, first, False, True)
    for e in range(1, nx):
        c_ir(e).wait_recv()
        unit(xof(e) * 2 + 1 - k, r, first, False, True)
    c_cy.wait_recv()
    block(z * 2 + 1 - y, gct)
    encode(gct[...], qy.at[0], my.at[0])

    def zstep(d, carry):
        @pl.when(d + 2 < nz)
        def _():
            c_cz(nz - 1 - d).wait_send()
            c_cz(nz - 2 - d).start()

        @pl.when(d + 1 < nz)
        def _():
            c_cz(nz - 1 - d).wait_recv()
            c_cr(d + 1).start()

        block(zof(d) * 2 + y, gco.at[d])
        c_cr(d).wait_recv()
        block(zof(d) * 2 + 1 - y, gct)
        encode(gct[...], qy.at[d], my.at[d])
        c_gy(d).start()

        @pl.when(d > 1)
        def _():
            flush(d - 1)

        return carry

    lax.fori_loop(1, nz, zstep, 0)
    c_gy(0).start()

    def rows_of(i):
        return pl.ds(pl.multiple_of(i * bi, bi), bi)

    def c_ik(e):
        return Both(
            rcopy(qk.at[e], rk.at[e], s_ik.at[e], r_ik.at[e], kpeer),
            rcopy(mk.at[e], nk.at[e], s_mk.at[e], r_mk.at[e], kpeer),
        )

    def c_xx(e):
        to, f = dev(z, y, xof(e), k), nx - e
        return Both(
            rcopy(qx.at[e], rx.at[f], s_xx.at[e], r_xx.at[f], to),
            rcopy(mx.at[e], nx_.at[f], s_mx.at[e], r_mx.at[f], to),
        )

    for e in list(range(1, nx)) + [0]:
        encode(gi[rows_of(xof(e) * 2 + 1 - k), :], qk.at[e], mk.at[e])
        c_ik(e).start()
    for e in range(1, nx):
        c_ik(e).wait_recv()
        encode(gi[rows_of(xof(e) * 2 + k), :] + decode(rk[e], nk[e]), qx.at[e], mx.at[e])
        c_xx(e).start()
    flush(nz - 1)

    c_ik(0).wait_recv()
    gi_out[...] = gi[rows_of(c), :] + decode(rk[0], nk[0])
    c_gy(0).wait_recv()
    gc_out[...] = gco[0] + decode(ry[0], ny[0])
    for e in range(1, nz):
        c_gz(nz - e).wait_recv()
        gc_out[...] += decode(rz[e], nz_[e])
    for e in range(1, nx):
        c_xx(nx - e).wait_recv()
        gi_out[...] += decode(rx[e], nx_[e])

    c_ic.wait_send()
    c_cy.wait_send()
    c_gy(0).wait_send()
    c_ik(0).wait_send()
    for e in range(1, nx):
        c_ix(e).wait_send()
        c_ir(e).wait_send()
        c_ik(e).wait_send()
        c_xx(e).wait_send()
    c_cz(1).wait_send()
    for e in range(1, nz):
        c_cr(e).wait_send()
        c_gy(e).wait_send()
        c_gz(e).wait_send()


def shards(nr, nc, items, contexts, tiles):
    bi, dim = items.shape
    bc = contexts.shape[0]
    nz, nx = nr // 2, nc // 2
    f32 = jnp.float32
    dma = pltpu.SemaphoreType.DMA
    pairs = [(), (nx,), (nx,), (), (nz,), (nz,), (nz,), (nz,), (nx,), (nx,)]
    pairs += [(nz,), (nz,), (nx,), (nx,)]
    sems = []
    for shape in pairs:
        sems += [dma(shape) if shape else dma] * 2
    vm = pl.BlockSpec(memory_space=pltpu.VMEM)
    return pl.pallas_call(
        functools.partial(kernel, nr, nc),
        out_shape=(
            jax.ShapeDtypeStruct((bi, dim), f32),
            jax.ShapeDtypeStruct((bc, dim), f32),
        ),
        in_specs=[vm, vm, pl.BlockSpec(memory_space=pltpu.SMEM)],
        out_specs=(vm, vm),
        scratch_shapes=[
            pltpu.VMEM((bi * nc, dim), items.dtype),
            pltpu.VMEM((bc * nr, dim), contexts.dtype),
            pltpu.VMEM((bi * nc, dim), f32),
            pltpu.VMEM((nz, bc, dim), f32),
            pltpu.VMEM((bc, dim), f32),
            pltpu.SMEM((2 * RB * CB,), f32),
        ]
        + [pltpu.VMEM((nz, bc, dim), jnp.int16)] * 4
        + [pltpu.VMEM((nx, bi, dim), jnp.int16)] * 4
        + [pltpu.VMEM((nz, 8, dim), f32)] * 4
        + [pltpu.VMEM((nx, 8, dim), f32)] * 4
        + sems,
        compiler_params=pltpu.CompilerParams(
            collective_id=0, has_side_effects=True, vmem_limit_bytes=40 * 2**20
        ),
    )(items, contexts, tiles)


def solution(mesh):
    nr, nc = mesh.shape["row"], mesh.shape["col"]
    placed = (P(("row", "col"), None), P(("col", "row"), None), P("row", "col", None, None))
    return jax.shard_map(
        functools.partial(shards, nr, nc),
        mesh=mesh,
        in_specs=placed,
        out_specs=(P(("row", "col"), None), P(("col", "row"), None)),
        check_vma=False,
    )
```

```python
import functools

import jax
import jax.numpy as jnp
from jax import lax
from jax.experimental import pallas as pl
from jax.experimental.pallas import tpu as pltpu
from jax.sharding import PartitionSpec as P

TILE = 1024
RB = 2
CB = 2
SLOTS = 4
LEVELS = 32766.0


class Both:
    def __init__(self, *copies):
        self.copies = copies

    def start(self):
        for one in self.copies:
            one.start()

    def wait_recv(self):
        for one in self.copies:
            one.wait_recv()

    def wait_send(self):
        for one in self.copies:
            one.wait_send()


def encode(value, codes, peaks):
    rows, dim = value.shape
    cube = value.reshape(rows // 8, 8, dim)
    peak = jnp.maximum(jnp.max(jnp.abs(cube), axis=0), 1e-30)
    peaks[...] = peak * (1.0 / LEVELS)
    scaled = jnp.round(cube * (LEVELS / peak)[None]).reshape(rows, dim)
    codes[...] = scaled.astype(jnp.int32).astype(jnp.int16)


def decode(codes, peaks):
    rows, dim = codes.shape
    cube = codes.astype(jnp.int32).astype(jnp.float32).reshape(rows // 8, 8, dim)
    return (cube * peaks[None]).reshape(rows, dim)


def kernel(
    nr, nc, items_ref, ctx_ref, tiles_ref, gi_out, gc_out,
    items_all, ctx_all, gi, gco, gct, coef,
    qy, ry, qz, rz, qk, rk, qx, rx, my, ny, mz, nz_, mk, nk, mx, nx_,
    s_ic, r_ic, s_ix, r_ix, s_ir, r_ir, s_cy, r_cy, s_cz, r_cz, s_cr, r_cr,
    s_gy, r_gy, s_gz, r_gz, s_ik, r_ik, s_xx, r_xx,
    s_my, r_my, s_mz, r_mz, s_mk, r_mk, s_mx, r_mx,
):
    nz, nx = nr // 2, nc // 2
    bi, bc = items_ref.shape[0], ctx_ref.shape[0]
    r = lax.axis_index("row")
    c = lax.axis_index("col")
    z, y = r // 2, r % 2
    x, k = c // 2, c % 2

    def dev(zz, yy, xx, kk):
        return (zz * 2 + yy, xx * 2 + kk)

    def zof(d):
        return lax.rem(z + d, nz)

    def xof(d):
        return lax.rem(x + d, nx)

    ypeer = dev(z, 1 - y, x, k)
    kpeer = dev(z, y, x, 1 - k)

    barrier = pltpu.get_barrier_semaphore()
    peers = [kpeer, ypeer]
    peers += [dev(z, y, xof(e), k) for e in range(1, nx)]
    peers += [dev(zof(e), y, x, k) for e in range(1, nz)]
    for p in peers:
        pl.semaphore_signal(barrier, inc=1, device_id=p, device_id_type=pl.DeviceIdType.MESH)
    pl.semaphore_wait(barrier, len(peers))

    def rcopy(src, dst, ss, rs, to):
        return pltpu.make_async_remote_copy(
            src_ref=src, dst_ref=dst, send_sem=ss, recv_sem=rs,
            device_id=to, device_id_type=pl.DeviceIdType.MESH,
        )

    def islot(i):
        return items_all.at[pl.ds(pl.multiple_of(i * bi, bi), bi)]

    def cslot(j):
        return ctx_all.at[pl.ds(pl.multiple_of(j * bc, bc), bc)]

    c_ic = rcopy(items_ref, islot(c), s_ic, r_ic, kpeer)
    c_cy = rcopy(ctx_ref, cslot(r), s_cy, r_cy, ypeer)

    def c_ix(e):
        return rcopy(items_ref, islot(c), s_ix.at[e], r_ix.at[nx - e], dev(z, y, xof(e), k))

    def dord(t):
        low, high = z, nz - 1 - z
        both = jnp.minimum(low, high)
        pair = ((t + 1) // 2) * (1 - 2 * ((t + 1) % 2))
        far = (t - both) * jnp.where(high > low, 1, -1)
        return lax.rem(jnp.where(t <= 2 * both, pair, far) + nz, nz)

    def c_line(zz, sign, sem, src=None):
        blk = cslot(zz * 2 + y)
        return rcopy(src if src is not None else blk, blk, s_cz.at[sem], r_cz.at[zz], dev(z + sign, y, x, k))

    def own_line(act):
        @pl.when(z < nz - 1)
        def _():
            act(c_line(z, 1, z, ctx_ref))

        @pl.when(z > 0)
        def _():
            act(c_line(z, -1, nz, ctx_ref))

    def pass_line(t, act):
        zz = zof(dord(t))

        @pl.when((zz < z) & (z < nz - 1))
        def _():
            act(c_line(zz, 1, zz))

        @pl.when((zz > z) & (z > 0))
        def _():
            act(c_line(zz, -1, zz))

    def arrive(t):
        d = dord(t)
        blk = cslot(zof(d) * 2 + y)
        rcopy(blk, blk, s_cz.at[zof(d)], r_cz.at[zof(d)], ypeer).wait_recv()
        pass_line(t, lambda copy: copy.start())
        c_cr(d).start()

    def c_ir(d):
        blk = islot(xof(d) * 2 + k)
        return rcopy(blk, blk, s_ir.at[d], r_ir.at[d], kpeer)

    def c_cr(d):
        blk = cslot(zof(d) * 2 + y)
        return rcopy(blk, blk, s_cr.at[d], r_cr.at[d], ypeer)

    for e in range(1, nx):
        c_ix(e).start()
    own_line(lambda copy: copy.start())
    c_cy.start()
    c_ic.start()

    items_all[pl.ds(pl.multiple_of(c * bi, bi), bi), :] = items_ref[...]
    ctx_all[pl.ds(pl.multiple_of(r * bc, bc), bc), :] = ctx_ref[...]

    for a in range(RB):
        for b in range(CB):
            pos = jnp.int32(0)
            neg = jnp.int32(0)
            for s in range(SLOTS):
                hit = (tiles_ref[0, 0, s, 0] == r * RB + a) & (tiles_ref[0, 0, s, 1] == c * CB + b)
                pos = pos + jnp.where(hit, tiles_ref[0, 0, s, 2], 0)
                neg = neg + jnp.where(hit, tiles_ref[0, 0, s, 3], 0)
            half = 0.5 / TILE**0.5
            coef[2 * (a * CB + b)] = (pos + neg).astype(jnp.float32) * half
            coef[2 * (a * CB + b) + 1] = (neg - pos).astype(jnp.float32) * half

    def unit(i, j, dst, first_c, first_i):
        cb = ctx_all[pl.ds(pl.multiple_of(j * bc, bc), bc), :]
        rows = pl.ds(pl.multiple_of(i * bi, bi), bi)
        ib = items_all[rows, :]
        at = 2 * ((i // (nc // RB)) * CB + j // (nr // CB))
        amp = coef[at]
        off = coef[at + 1]
        sc = lax.dot_general(ib, cb, (((1,), (1,)), ((), ())), preferred_element_type=jnp.float32)
        res = (jnp.tanh(sc * 0.5) * amp + off).astype(jnp.bfloat16)
        it = jnp.dot(res, cb, preferred_element_type=jnp.float32)
        ct = lax.dot_general(res, ib, (((0,), (0,)), ((), ())), preferred_element_type=jnp.float32)
        if first_i:
            gi[rows, :] = it
        else:
            gi[rows, :] += it
        if first_c:
            dst[...] = ct
        else:
            dst[...] += ct

    def block(j, dst, first_i=False):
        unit(c, j, dst, True, first_i)
        unit(x * 2 + 1 - k, j, dst, False, first_i)

        def step(e, carry):
            unit(xof(e) * 2 + k, j, dst, False, first_i)
            unit(xof(e) * 2 + 1 - k, j, dst, False, first_i)
            return carry

        lax.fori_loop(1, nx, step, 0, unroll=nx <= 2)

    def c_gy(d):
        return Both(
            rcopy(qy.at[d], ry.at[d], s_gy.at[d], r_gy.at[d], ypeer),
            rcopy(my.at[d], ny.at[d], s_my.at[d], r_my.at[d], ypeer),
        )

    def c_gz(d):
        to, e = dev(zof(d), y, x, k), nz - d
        return Both(
            rcopy(qz.at[d], rz.at[e], s_gz.at[d], r_gz.at[e], to),
            rcopy(mz.at[d], nz_.at[e], s_mz.at[d], r_mz.at[e], to),
        )

    def flush(d):
        c_gy(d).wait_recv()
        encode(gco[d] + decode(ry[d], ny[d]), qz.at[d], mz.at[d])
        c_gz(d).start()

    first = gco.at[0]
    unit(c, r, first, True, True)
    c_ic.wait_recv()
    unit(x * 2 + 1 - k, r, first, False, True)
    for t in range(1, min(nz, 3)):
        arrive(t)
    for e in range(1, nx):
        c_ix(nx - e).wait_recv()
        c_ir(e).start()
        unit(xof(e) * 2 + k, r, first, False, True)
    for e in range(1, nx):
        c_ir(e).wait_recv()
        unit(xof(e) * 2 + 1 - k, r, first, False, True)
    c_cy.wait_recv()
    block(z * 2 + 1 - y, gct)
    encode(gct[...], qy.at[0], my.at[0])

    def zstep(t, carry):
        d = dord(t)

        @pl.when(t + 2 < nz)
        def _():
            arrive(t + 2)

        block(zof(d) * 2 + y, gco.at[d])
        c_cr(d).wait_recv()
        block(zof(d) * 2 + 1 - y, gct)
        encode(gct[...], qy.at[d], my.at[d])
        c_gy(d).start()

        @pl.when(t > 1)
        def _():
            flush(dord(t - 1))

        return carry

    lax.fori_loop(1, nz, zstep, 0)
    c_gy(0).start()

    def rows_of(i):
        return pl.ds(pl.multiple_of(i * bi, bi), bi)

    def c_ik(e):
        return Both(
            rcopy(qk.at[e], rk.at[e], s_ik.at[e], r_ik.at[e], kpeer),
            rcopy(mk.at[e], nk.at[e], s_mk.at[e], r_mk.at[e], kpeer),
        )

    def c_xx(e):
        to, f = dev(z, y, xof(e), k), nx - e
        return Both(
            rcopy(qx.at[e], rx.at[f], s_xx.at[e], r_xx.at[f], to),
            rcopy(mx.at[e], nx_.at[f], s_mx.at[e], r_mx.at[f], to),
        )

    for e in list(range(1, nx)) + [0]:
        encode(gi[rows_of(xof(e) * 2 + 1 - k), :], qk.at[e], mk.at[e])
        c_ik(e).start()
    for e in range(1, nx):
        c_ik(e).wait_recv()
        encode(gi[rows_of(xof(e) * 2 + k), :] + decode(rk[e], nk[e]), qx.at[e], mx.at[e])
        c_xx(e).start()
    flush(dord(nz - 1))

    c_ik(0).wait_recv()
    gi_out[...] = gi[rows_of(c), :] + decode(rk[0], nk[0])
    c_gy(0).wait_recv()
    gc_out[...] = gco[0] + decode(ry[0], ny[0])
    for e in range(1, nz):
        c_gz(nz - e).wait_recv()
        gc_out[...] += decode(rz[e], nz_[e])
    for e in range(1, nx):
        c_xx(nx - e).wait_recv()
        gi_out[...] += decode(rx[e], nx_[e])

    c_ic.wait_send()
    c_cy.wait_send()
    c_gy(0).wait_send()
    c_ik(0).wait_send()
    for e in range(1, nx):
        c_ix(e).wait_send()
        c_ir(e).wait_send()
        c_ik(e).wait_send()
        c_xx(e).wait_send()
    own_line(lambda copy: copy.wait_send())
    for t in range(1, nz):
        pass_line(t, lambda copy: copy.wait_send())
    for e in range(1, nz):
        c_cr(e).wait_send()
        c_gy(e).wait_send()
        c_gz(e).wait_send()


def shards(nr, nc, items, contexts, tiles):
    bi, dim = items.shape
    bc = contexts.shape[0]
    nz, nx = nr // 2, nc // 2
    f32 = jnp.float32
    dma = pltpu.SemaphoreType.DMA
    pairs = [(), (nx,), (nx,), (), (nz + 1,), (nz,), (nz,), (nz,), (nx,), (nx,)]
    pairs += [(nz,), (nz,), (nx,), (nx,)]
    sems = []
    for shape in pairs:
        sems += [dma(shape) if shape else dma] * 2
    vm = pl.BlockSpec(memory_space=pltpu.VMEM)
    return pl.pallas_call(
        functools.partial(kernel, nr, nc),
        out_shape=(
            jax.ShapeDtypeStruct((bi, dim), f32),
            jax.ShapeDtypeStruct((bc, dim), f32),
        ),
        in_specs=[vm, vm, pl.BlockSpec(memory_space=pltpu.SMEM)],
        out_specs=(vm, vm),
        scratch_shapes=[
            pltpu.VMEM((bi * nc, dim), items.dtype),
            pltpu.VMEM((bc * nr, dim), contexts.dtype),
            pltpu.VMEM((bi * nc, dim), f32),
            pltpu.VMEM((nz, bc, dim), f32),
            pltpu.VMEM((bc, dim), f32),
            pltpu.SMEM((2 * RB * CB,), f32),
        ]
        + [pltpu.VMEM((nz, bc, dim), jnp.int16)] * 4
        + [pltpu.VMEM((nx, bi, dim), jnp.int16)] * 4
        + [pltpu.VMEM((nz, 8, dim), f32)] * 4
        + [pltpu.VMEM((nx, 8, dim), f32)] * 4
        + sems,
        compiler_params=pltpu.CompilerParams(
            collective_id=0, has_side_effects=True, vmem_limit_bytes=40 * 2**20
        ),
    )(items, contexts, tiles)


def solution(mesh):
    nr, nc = mesh.shape["row"], mesh.shape["col"]
    placed = (P(("row", "col"), None), P(("col", "row"), None), P("row", "col", None, None))
    return jax.shard_map(
        functools.partial(shards, nr, nc),
        mesh=mesh,
        in_specs=placed,
        out_specs=(P(("row", "col"), None), P(("col", "row"), None)),
        check_vma=False,
    )
```

```python
import functools

import jax
import jax.numpy as jnp
from jax import lax
from jax.experimental import pallas as pl
from jax.experimental.pallas import tpu as pltpu
from jax.sharding import PartitionSpec as P

TILE = 1024
RB = 2
CB = 2
SLOTS = 4
LEVELS = 32766.0


class Both:
    def __init__(self, *copies):
        self.copies = copies

    def start(self):
        for one in self.copies:
            one.start()

    def wait_recv(self):
        for one in self.copies:
            one.wait_recv()

    def wait_send(self):
        for one in self.copies:
            one.wait_send()


def encode(value, codes, peaks):
    rows, dim = value.shape
    cube = value.reshape(rows // 8, 8, dim)
    peak = jnp.maximum(jnp.max(jnp.abs(cube), axis=0), 1e-30)
    peaks[...] = peak * (1.0 / LEVELS)
    scaled = jnp.round(cube * (LEVELS / peak)[None]).reshape(rows, dim)
    codes[...] = scaled.astype(jnp.int32).astype(jnp.int16)


def decode(codes, peaks):
    rows, dim = codes.shape
    cube = codes.astype(jnp.int32).astype(jnp.float32).reshape(rows // 8, 8, dim)
    return (cube * peaks[None]).reshape(rows, dim)


def kernel(
    nr, nc, items_ref, ctx_ref, tiles_ref, gi_out, gc_out,
    items_all, ctx_all, gi, gco, gct, coef,
    qy, ry, qz, rz, qk, rk, qx, rx, my, ny, mz, nz_, mk, nk, mx, nx_,
    s_ic, r_ic, s_ix, r_ix, s_ir, r_ir, s_cy, r_cy, s_cz, r_cz, s_cr, r_cr,
    s_gy, r_gy, s_gz, r_gz, s_ik, r_ik, s_xx, r_xx,
    s_my, r_my, s_mz, r_mz, s_mk, r_mk, s_mx, r_mx,
):
    nz, nx = nr // 2, nc // 2
    bi, bc = items_ref.shape[0], ctx_ref.shape[0]
    r = lax.axis_index("row")
    c = lax.axis_index("col")
    z, y = r // 2, r % 2
    x, k = c // 2, c % 2

    def dev(zz, yy, xx, kk):
        return (zz * 2 + yy, xx * 2 + kk)

    def zof(d):
        return lax.rem(z + d, nz)

    def xof(d):
        return lax.rem(x + d, nx)

    ypeer = dev(z, 1 - y, x, k)
    kpeer = dev(z, y, x, 1 - k)

    barrier = pltpu.get_barrier_semaphore()
    peers = [kpeer, ypeer]
    peers += [dev(z, y, xof(e), k) for e in range(1, nx)]
    peers += [dev(zof(e), y, x, k) for e in range(1, nz)]
    for p in peers:
        pl.semaphore_signal(barrier, inc=1, device_id=p, device_id_type=pl.DeviceIdType.MESH)
    pl.semaphore_wait(barrier, len(peers))

    def rcopy(src, dst, ss, rs, to):
        return pltpu.make_async_remote_copy(
            src_ref=src, dst_ref=dst, send_sem=ss, recv_sem=rs,
            device_id=to, device_id_type=pl.DeviceIdType.MESH,
        )

    def islot(i):
        return items_all.at[pl.ds(pl.multiple_of(i * bi, bi), bi)]

    def cslot(j):
        return ctx_all.at[pl.ds(pl.multiple_of(j * bc, bc), bc)]

    c_ic = rcopy(items_ref, islot(c), s_ic, r_ic, kpeer)
    c_cy = rcopy(ctx_ref, cslot(r), s_cy, r_cy, ypeer)

    def c_ix(e):
        return rcopy(items_ref, islot(c), s_ix.at[e], r_ix.at[nx - e], dev(z, y, xof(e), k))

    def c_cz(e):
        return rcopy(ctx_ref, cslot(r), s_cz.at[e], r_cz.at[nz - e], dev(zof(e), y, x, k))

    def c_ir(d):
        blk = islot(xof(d) * 2 + k)
        return rcopy(blk, blk, s_ir.at[d], r_ir.at[d], kpeer)

    def c_cr(d):
        blk = cslot(zof(d) * 2 + y)
        return rcopy(blk, blk, s_cr.at[d], r_cr.at[d], ypeer)

    for e in range(1, nx):
        c_ix(e).start()
    c_cz(nz - 1).start()
    c_cy.start()
    c_ic.start()

    items_all[pl.ds(pl.multiple_of(c * bi, bi), bi), :] = items_ref[...]
    ctx_all[pl.ds(pl.multiple_of(r * bc, bc), bc), :] = ctx_ref[...]

    for a in range(RB):
        for b in range(CB):
            pos = jnp.int32(0)
            neg = jnp.int32(0)
            for s in range(SLOTS):
                hit = (tiles_ref[0, 0, s, 0] == r * RB + a) & (tiles_ref[0, 0, s, 1] == c * CB + b)
                pos = pos + jnp.where(hit, tiles_ref[0, 0, s, 2], 0)
                neg = neg + jnp.where(hit, tiles_ref[0, 0, s, 3], 0)
            half = 0.5 / TILE**0.5
            coef[2 * (a * CB + b)] = (pos + neg).astype(jnp.float32) * half
            coef[2 * (a * CB + b) + 1] = (neg - pos).astype(jnp.float32) * half

    def unit(i, j, dst, first_c, first_i):
        cb = ctx_all[pl.ds(pl.multiple_of(j * bc, bc), bc), :]
        rows = pl.ds(pl.multiple_of(i * bi, bi), bi)
        ib = items_all[rows, :]
        at = 2 * ((i // (nc // RB)) * CB + j // (nr // CB))
        amp = coef[at]
        off = coef[at + 1]
        sc = lax.dot_general(ib, cb, (((1,), (1,)), ((), ())), preferred_element_type=jnp.float32)
        res = (jnp.tanh(sc * 0.5) * amp + off).astype(jnp.bfloat16)
        it = jnp.dot(res, cb, preferred_element_type=jnp.float32)
        ct = lax.dot_general(res, ib, (((0,), (0,)), ((), ())), preferred_element_type=jnp.float32)
        if first_i:
            gi[rows, :] = it
        else:
            gi[rows, :] += it
        if first_c:
            dst[...] = ct
        else:
            dst[...] += ct

    def block(j, dst, first_i=False):
        unit(c, j, dst, True, first_i)
        unit(x * 2 + 1 - k, j, dst, False, first_i)

        def step(e, carry):
            unit(xof(e) * 2 + k, j, dst, False, first_i)
            unit(xof(e) * 2 + 1 - k, j, dst, False, first_i)
            return carry

        lax.fori_loop(1, nx, step, 0, unroll=nx <= 2)

    def c_gy(d):
        return Both(
            rcopy(qy.at[d], ry.at[d], s_gy.at[d], r_gy.at[d], ypeer),
            rcopy(my.at[d], ny.at[d], s_my.at[d], r_my.at[d], ypeer),
        )

    def c_gz(d):
        to, e = dev(zof(d), y, x, k), nz - d
        return Both(
            rcopy(qz.at[d], rz.at[e], s_gz.at[d], r_gz.at[e], to),
            rcopy(mz.at[d], nz_.at[e], s_mz.at[d], r_mz.at[e], to),
        )

    def flush(d):
        c_gy(d).wait_recv()
        encode(gco[d] + decode(ry[d], ny[d]), qz.at[d], mz.at[d])
        c_gz(d).start()

    first = gco.at[0]
    unit(c, r, first, True, True)
    c_ic.wait_recv()
    unit(x * 2 + 1 - k, r, first, False, True)
    c_cz(nz - 1).wait_send()
    if nz > 2:
        c_cz(nz - 2).start()
    c_cz(nz - 1).wait_recv()
    c_cr(1).start()
    for e in range(1, nx):
        c_ix(nx - e).wait_recv()
        c_ir(e).start()
        unit(xof(e) * 2 + k, r, first, False, True)
    for e in range(1, nx):
        c_ir(e).wait_recv()
        unit(xof(e) * 2 + 1 - k, r, first, False, True)
    c_cy.wait_recv()
    block(z * 2 + 1 - y, gct)
    encode(gct[...], qy.at[0], my.at[0])

    def zstep(d, carry):
        @pl.when(d + 2 < nz)
        def _():
            c_cz(nz - 1 - d).wait_send()
            c_cz(nz - 2 - d).start()

        @pl.when(d + 1 < nz)
        def _():
            c_cz(nz - 1 - d).wait_recv()
            c_cr(d + 1).start()

        block(zof(d) * 2 + y, gco.at[d])
        c_cr(d).wait_recv()

        @pl.when(d == nz - 1)
        def _():
            c_gy(0).start()

        block(zof(d) * 2 + 1 - y, gct)
        encode(gct[...], qy.at[d], my.at[d])
        c_gy(d).start()

        @pl.when(d > 1)
        def _():
            flush(d - 1)

        return carry

    lax.fori_loop(1, nz, zstep, 0)

    def rows_of(i):
        return pl.ds(pl.multiple_of(i * bi, bi), bi)

    def c_ik(e):
        return Both(
            rcopy(qk.at[e], rk.at[e], s_ik.at[e], r_ik.at[e], kpeer),
            rcopy(mk.at[e], nk.at[e], s_mk.at[e], r_mk.at[e], kpeer),
        )

    def c_xx(e):
        to, f = dev(z, y, xof(e), k), nx - e
        return Both(
            rcopy(qx.at[e], rx.at[f], s_xx.at[e], r_xx.at[f], to),
            rcopy(mx.at[e], nx_.at[f], s_mx.at[e], r_mx.at[f], to),
        )

    for e in list(range(1, nx)) + [0]:
        encode(gi[rows_of(xof(e) * 2 + 1 - k), :], qk.at[e], mk.at[e])
        c_ik(e).start()
    for e in range(1, nx):
        c_ik(e).wait_recv()
        encode(gi[rows_of(xof(e) * 2 + k), :] + decode(rk[e], nk[e]), qx.at[e], mx.at[e])
        c_xx(e).start()
    flush(nz - 1)

    c_ik(0).wait_recv()
    gi_out[...] = gi[rows_of(c), :] + decode(rk[0], nk[0])
    c_gy(0).wait_recv()
    gc_out[...] = gco[0] + decode(ry[0], ny[0])
    for e in range(1, nz):
        c_gz(nz - e).wait_recv()
        gc_out[...] += decode(rz[e], nz_[e])
    for e in range(1, nx):
        c_xx(nx - e).wait_recv()
        gi_out[...] += decode(rx[e], nx_[e])

    c_ic.wait_send()
    c_cy.wait_send()
    c_gy(0).wait_send()
    c_ik(0).wait_send()
    for e in range(1, nx):
        c_ix(e).wait_send()
        c_ir(e).wait_send()
        c_ik(e).wait_send()
        c_xx(e).wait_send()
    c_cz(1).wait_send()
    for e in range(1, nz):
        c_cr(e).wait_send()
        c_gy(e).wait_send()
        c_gz(e).wait_send()


def shards(nr, nc, items, contexts, tiles):
    bi, dim = items.shape
    bc = contexts.shape[0]
    nz, nx = nr // 2, nc // 2
    f32 = jnp.float32
    dma = pltpu.SemaphoreType.DMA
    pairs = [(), (nx,), (nx,), (), (nz,), (nz,), (nz,), (nz,), (nx,), (nx,)]
    pairs += [(nz,), (nz,), (nx,), (nx,)]
    sems = []
    for shape in pairs:
        sems += [dma(shape) if shape else dma] * 2
    vm = pl.BlockSpec(memory_space=pltpu.VMEM)
    return pl.pallas_call(
        functools.partial(kernel, nr, nc),
        out_shape=(
            jax.ShapeDtypeStruct((bi, dim), f32),
            jax.ShapeDtypeStruct((bc, dim), f32),
        ),
        in_specs=[vm, vm, pl.BlockSpec(memory_space=pltpu.SMEM)],
        out_specs=(vm, vm),
        scratch_shapes=[
            pltpu.VMEM((bi * nc, dim), items.dtype),
            pltpu.VMEM((bc * nr, dim), contexts.dtype),
            pltpu.VMEM((bi * nc, dim), f32),
            pltpu.VMEM((nz, bc, dim), f32),
            pltpu.VMEM((bc, dim), f32),
            pltpu.SMEM((2 * RB * CB,), f32),
        ]
        + [pltpu.VMEM((nz, bc, dim), jnp.int16)] * 4
        + [pltpu.VMEM((nx, bi, dim), jnp.int16)] * 4
        + [pltpu.VMEM((nz, 8, dim), f32)] * 4
        + [pltpu.VMEM((nx, 8, dim), f32)] * 4
        + sems,
        compiler_params=pltpu.CompilerParams(
            collective_id=0, has_side_effects=True, vmem_limit_bytes=40 * 2**20
        ),
    )(items, contexts, tiles)


def solution(mesh):
    nr, nc = mesh.shape["row"], mesh.shape["col"]
    placed = (P(("row", "col"), None), P(("col", "row"), None), P("row", "col", None, None))
    return jax.shard_map(
        functools.partial(shards, nr, nc),
        mesh=mesh,
        in_specs=placed,
        out_specs=(P(("row", "col"), None), P(("col", "row"), None)),
        check_vma=False,
    )
```
